32 devices in a mesh: layer: 2 (over x), latent: 8 (over z, y), tok: 2 (over core).
Axes of the slice: x: 2, y: 2, z: 4, core: 2. Of those that a mesh axis runs over, the one named last changes fastest.
Arguments:
- activations: bfloat16 [2, 1280, 3584], P('layer', 'tok'), may hold values from -6 to 6
- enc_weight: bfloat16 [2, 3584, 8192], P('layer', 'tok', 'latent'), may hold values from -0.0625 to 0.0625
- enc_bias: float32 [8192], P('latent'), may hold values from -3 to 3
- dec_weight: bfloat16 [8192, 2, 3584], P('latent', 'layer', 'tok'), may hold values from -0.110485435 to 0.110485435
- dec_bias: float32 [2, 3584], P('layer'), may hold values from -3 to 3
Outputs:
- grad_enc: bfloat16 [2, 3584, 8192], P('layer', 'tok', 'latent')
- grad_dec: bfloat16 [8192, 2, 3584], P('latent', 'layer', 'tok')
The draws below stay inside these ranges and needn't reach their ends.
All inputs are finite; a program needn't handle non-finite values.
Results may differ from the reference program's by a relative error of at most 0.023.
Values may be sent and summed in bfloat16 or wider, within the bound.
A program may use at most 128 MiB of HBM per device.

```python
import jax
import jax.numpy as jnp
from jax import lax

D = 3584
LAYERS = 2
LATENTS = 8192
TOKENS = 1280
N_TOK = 2


def draw_dec_weight(key, part):
    blocks = LAYERS * N_TOK
    width_part = D // N_TOK
    layer_pos = jnp.arange(LAYERS, dtype=jnp.float32)[:, None]
    feature_pos = (jnp.arange(D) // width_part).astype(jnp.float32)[None, :]
    block_rank = layer_pos * N_TOK + feature_pos
    ratio = 3.3
    noise = jax.random.normal(jax.random.fold_in(key, 17), (LATENTS, LAYERS, D), jnp.float32)
    scales = jnp.exp(jnp.log(ratio) * block_rank / max(blocks - 1, 1))
    ranks = jnp.arange(blocks, dtype=jnp.float32)
    mean_square = jnp.mean(jnp.exp(2.0 * jnp.log(ratio) * ranks / max(blocks - 1, 1)))
    scales = scales / jnp.sqrt(mean_square)
    values = noise * scales[None] / jnp.sqrt(jnp.float32(LATENTS))
    limit = 10.0 / jnp.sqrt(jnp.float32(LATENTS))
    return jnp.clip(values, -limit, limit).astype(jnp.bfloat16)


def levels(rng, extent, shards, least, top_value):
    loudness, own = 1.0, jax.random.fold_in(rng, 6)
    for axis_at, shards_of in shards:
        draws = jnp.exp(jax.random.uniform(jax.random.fold_in(own, axis_at), (shards_of,), jnp.float32, least / len(shards), top_value / len(shards)))
        loudness = loudness * jnp.repeat(draws, extent[axis_at] // shards_of).reshape([-1 if axis == axis_at else 1 for axis in range(len(extent))])
    return loudness


def normal_values(key, dims, width, most, shards=(), held_as=jnp.bfloat16):
    loudness = levels(key, dims, shards, -0.22, 0.18) if shards else 1.0
    array = jax.random.normal(key, dims, jnp.float32) * width * loudness
    return jnp.minimum(jnp.maximum(array, -most), most).astype(held_as)


def setup_inputs(seed: int = 0) -> dict:
    splits = jax.random.split(jax.random.key(seed), 6)
    return {
        "activations": normal_values(splits[0], (LAYERS, TOKENS, D), 1.0, 6.0, ((0, 2), (1, 2))),
        "enc_weight": normal_values(splits[1], (LAYERS, D, LATENTS), (LAYERS * D) ** -0.5, 0.0625, ((0, 2), (1, 2), (2, 8))),
        "enc_bias": normal_values(splits[2], (LATENTS,), 0.5, 3.0, ((0, 8),), jnp.float32),
        "dec_weight": draw_dec_weight(jax.random.fold_in(splits[5], 71), 0),
        "dec_bias": normal_values(splits[4], (LAYERS, D), 0.5, 3.0, ((0, 2),), jnp.float32),
    }


LAMBDA = 1.0
EPSILON = 1e-06

def reference(activations, enc_weight, enc_bias, dec_weight, dec_bias):
    dec_norms = jnp.sqrt(lax.optimization_barrier(jnp.sum(jnp.square(dec_weight.astype(jnp.float32)), axis=(1, 2))) + EPSILON)
    preact = enc_bias
    for layer_idx in range(LAYERS):
        preact = preact + jnp.dot(activations[layer_idx], enc_weight[layer_idx], preferred_element_type=jnp.float32)
    positive = jnp.maximum(preact, 0.0)
    latents = (positive * positive).astype(jnp.bfloat16)
    loss_scale = 1.0 / jnp.sqrt(jnp.float32(TOKENS))
    errors_list = []
    back_proj = jnp.zeros(preact.shape, jnp.float32)
    for layer_idx in range(LAYERS):
        rebuilt = jnp.dot(latents, dec_weight[:, layer_idx, :], preferred_element_type=jnp.float32) + dec_bias[layer_idx]
        recon_error = (rebuilt - activations[layer_idx].astype(jnp.float32)).astype(jnp.bfloat16)
        errors_list.append(recon_error)
        back_proj = back_proj + lax.dot_general(recon_error, dec_weight[:, layer_idx, :], (((1,), (1,)), ((), ())), preferred_element_type=jnp.float32)
    pre_grad = (loss_scale * (back_proj + LAMBDA * dec_norms) * 2.0 * positive).astype(jnp.bfloat16)
    half_rows = TOKENS // N_TOK
    enc_layers = []
    dec_layers = []
    for layer_idx in range(LAYERS):
        enc_total = jnp.zeros((activations.shape[2], latents.shape[1]), jnp.float32)
        dec_total = jnp.zeros((latents.shape[1], activations.shape[2]), jnp.float32)
        dec_matrix = dec_weight[:, layer_idx, :].astype(jnp.float32)
        for half_idx in range(N_TOK):
            lower = half_idx * half_rows
            part_rows = activations[layer_idx, lower:lower + half_rows]
            part_grad = pre_grad[lower:lower + half_rows]
            part_lat = latents[lower:lower + half_rows]
            part_err = errors_list[layer_idx][lower:lower + half_rows]
            enc_part = lax.dot_general(part_rows, part_grad, (((0,), (0,)), ((), ())), preferred_element_type=jnp.float32)
            enc_total = enc_total + lax.optimization_barrier(enc_part.astype(jnp.bfloat16)).astype(jnp.float32)
            col_totals = lax.optimization_barrier(jnp.sum(part_lat.astype(jnp.float32), axis=0))
            dec_part = loss_scale * (lax.dot_general(part_lat, part_err, (((0,), (0,)), ((), ())), preferred_element_type=jnp.float32) + LAMBDA * col_totals[:, None] * dec_matrix / dec_norms[:, None])
            dec_total = dec_total + lax.optimization_barrier(dec_part.astype(jnp.bfloat16)).astype(jnp.float32)
        enc_layers.append(enc_total.astype(jnp.bfloat16))
        dec_layers.append(dec_total.astype(jnp.bfloat16))
    grad_enc = jnp.stack(enc_layers, axis=0)
    grad_dec = jnp.stack(dec_layers, axis=1)
    return (grad_enc, grad_dec)
```

```python
import math

import jax
import jax.numpy as jnp
from jax import lax
from jax.sharding import PartitionSpec as P

LAMBDA = 1.0
EPSILON = 1e-06


def dot(a, b, dims):
    return lax.dot_general(a, b, (dims, ((), ())), preferred_element_type=jnp.float32)


def swap(x, axis):
    return lax.ppermute(x, axis, [(0, 1), (1, 0)])


def latent_sum(part):
    return lax.psum(part, "latent")


def on_device(activations, enc_weight, enc_bias, dec_weight, dec_bias):
    f32, bf16 = jnp.float32, jnp.bfloat16
    rows = activations[0]
    row_count = rows.shape[0]
    loss_scale = 1.0 / math.sqrt(row_count * lax.axis_size("tok"))
    enc, dec = enc_weight[0], dec_weight[:, 0, :]
    width = enc.shape[0]
    tok = lax.axis_index("tok")
    act_own = lax.dynamic_slice_in_dim(rows, tok * width, width, axis=1)
    act_sent = lax.dynamic_slice_in_dim(rows, (1 - tok) * width, width, axis=1)
    act_other = swap(act_sent, "tok")
    half_sq = jnp.sum(jnp.square(dec.astype(f32)), axis=1)
    dec_norms = jnp.sqrt(lax.psum(half_sq, ("layer", "tok")) + EPSILON)

    def token_terms(own, other):
        arrived = swap(other.astype(bf16), "tok")
        mine = (own + arrived.astype(f32)).astype(bf16)
        return mine.astype(f32) + swap(mine, "layer").astype(f32)

    pre_other = dot(act_other, enc, ((1,), (0,)))
    pre_own = dot(act_own, enc, ((1,), (0,)))
    preact = token_terms(pre_own, pre_other) + enc_bias
    positive = jnp.maximum(preact, 0.0)
    lat_own = (positive * positive).astype(bf16)
    lat_other = swap(lat_own, "tok")
    bias = lax.dynamic_slice_in_dim(dec_bias[0], tok * width, width, axis=0)

    def error(lat, act):
        part = dot(lat, dec, ((1,), (0,))).astype(bf16)
        return (latent_sum(part).astype(f32) + bias - act.astype(f32)).astype(bf16)

    err_own = error(lat_own, act_own)
    err_other = error(lat_other, act_other)
    back_other = dot(err_other, dec, ((1,), (1,)))
    back_own = dot(err_own, dec, ((1,), (1,)))
    back_proj = token_terms(back_own, back_other)
    grad_own = (loss_scale * (back_proj + LAMBDA * dec_norms) * 2.0 * positive).astype(bf16)
    grad_other = swap(grad_own, "tok")
    grad_enc = dot(act_own, grad_own, ((0,), (0,))) + dot(act_other, grad_other, ((0,), (0,)))
    col_totals = jnp.sum(lat_own.astype(f32), axis=0) + jnp.sum(lat_other.astype(f32), axis=0)
    grad_dec = loss_scale * (
        dot(lat_own, err_own, ((0,), (0,)))
        + dot(lat_other, err_other, ((0,), (0,)))
        + (LAMBDA * col_totals / dec_norms)[:, None] * dec.astype(f32)
    )
    return grad_enc.astype(bf16)[None], grad_dec.astype(bf16)[:, None, :]


def solution(mesh):
    placed = (
        P("layer", "tok", None),
        P("layer", "tok", "latent"),
        P("latent"),
        P("latent", "layer", "tok"),
        P("layer", None),
    )
    return jax.shard_map(
        on_device,
        mesh=mesh,
        in_specs=placed,
        out_specs=(P("layer", "tok", "latent"), P("latent", "layer", "tok")),
        check_vma=False,
    )
```

```python
import functools
import math

import jax
import jax.numpy as jnp
from jax import lax
from jax.experimental import pallas as pl
from jax.experimental.pallas import tpu as pltpu
from jax.sharding import PartitionSpec as P

LAMBDA = 1.0
EPSILON = 1e-06


def dot(a, b, dims):
    return lax.dot_general(a, b, (dims, ((), ())), preferred_element_type=jnp.float32)


def swap(x, axis):
    return lax.ppermute(x, axis, [(0, 1), (1, 0)])


def ring_kernel(
    n, lat0, lat1, act0, act1, dec, bias, err0, err1, back0, back1,
    slots, rs_send, rs_recv, ag_send, ag_recv,
):
    lats, acts, errs, backs = (lat0, lat1), (act0, act1), (err0, err1), (back0, back1)
    half = n // 2
    latent = lax.axis_index("latent")
    odd = lax.rem(latent, 2)
    place = lax.div(latent, 2) + odd * (n - 1 - 2 * lax.div(latent, 2))

    def device_at(spot):
        far = lax.div(spot, half)
        return (1 - far) * 2 * spot + far * (2 * (n - 1 - spot) + 1)

    right = device_at(lax.rem(place + 1, n))
    left = device_at(lax.rem(place + n - 1, n))
    targets = (right, left)

    def chunk(way, step):
        return lax.rem(place - step + 2 * n, n) if way == 0 else lax.rem(place + step + n, n)

    def rs_copy(way, step):
        return pltpu.make_async_remote_copy(
            src_ref=slots.at[way, step],
            dst_ref=slots.at[way, step + 1],
            send_sem=rs_send.at[way, step],
            recv_sem=rs_recv.at[way, step],
            device_id={"latent": targets[way]},
            device_id_type=pl.DeviceIdType.MESH,
        )

    def ag_copy(way, step, held):
        return pltpu.make_async_remote_copy(
            src_ref=errs[way].at[held],
            dst_ref=errs[way].at[held],
            send_sem=ag_send.at[way, step],
            recv_sem=ag_recv.at[way, step],
            device_id={"latent": targets[way]},
            device_id_type=pl.DeviceIdType.MESH,
        )

    def partial(way, step):
        return jnp.dot(lats[way][chunk(way, step)], dec[...], preferred_element_type=jnp.float32)

    def project(way, held):
        out = dot(errs[way][held], dec[...], ((1,), (1,)))
        backs[way][held] = out.astype(backs[way].dtype)

    barrier = pltpu.get_barrier_semaphore()
    for target in targets:
        pl.semaphore_signal(
            barrier, inc=1, device_id={"latent": target}, device_id_type=pl.DeviceIdType.MESH
        )
    for way in range(2):
        slots[way, 0] = partial(way, 0).astype(slots.dtype)
    pl.semaphore_wait(barrier, 2)
    for way in range(2):
        rs_copy(way, 0).start()

    @pl.loop(1, n - 1)
    def _(step):
        parts = [partial(way, step) for way in range(2)]
        for way in range(2):
            rs_copy(way, step - 1).wait_recv()
            total = slots[way, step].astype(jnp.float32) + parts[way]
            slots[way, step] = total.astype(slots.dtype)
            rs_copy(way, step).start()

    parts = [partial(way, n - 1) for way in range(2)]
    for way in range(2):
        held = chunk(way, n - 1)
        rs_copy(way, n - 2).wait_recv()
        total = slots[way, n - 1].astype(jnp.float32) + parts[way]
        error = total + bias[...] - acts[way][held].astype(jnp.float32)
        errs[way][held] = error.astype(errs[way].dtype)
        ag_copy(way, 0, held).start()
    for way in range(2):
        project(way, chunk(way, n - 1))

    @pl.loop(0, n - 2)
    def _(step):
        for way in range(2):
            ag_copy(way, step, chunk(way, step)).wait_recv()
            ag_copy(way, step + 1, chunk(way, step)).start()
        for way in range(2):
            project(way, chunk(way, step))

    for way in range(2):
        ag_copy(way, n - 2, chunk(way, n - 2)).wait_recv()
    for way in range(2):
        project(way, chunk(way, n - 2))

    @pl.loop(0, n - 1)
    def _(step):
        for way in range(2):
            rs_copy(way, step).wait_send()
            ag_copy(way, step, chunk(way, step - 1 + n)).wait_send()


def error_and_back(lat_own, lat_other, act_own, act_other, dec, bias):
    n = lax.axis_size("latent")
    rows, latents = lat_own.shape
    width = dec.shape[1]
    part = rows // n
    cut = lambda x: x.reshape(n, part, x.shape[1])
    shape = jax.ShapeDtypeStruct
    errs = [shape((n, part, width), jnp.bfloat16)] * 2
    backs = [shape((n, part, latents), jnp.float32), shape((n, part, latents), jnp.bfloat16)]
    sems = pltpu.SemaphoreType.DMA((2, n - 1))
    outs = pl.pallas_call(
        functools.partial(ring_kernel, n),
        out_shape=errs + backs,
        in_specs=[pl.BlockSpec(memory_space=pltpu.VMEM)] * 6,
        out_specs=[pl.BlockSpec(memory_space=pltpu.VMEM)] * 4,
        scratch_shapes=[pltpu.VMEM((2, n, part, width), jnp.bfloat16), sems, sems, sems, sems],
        compiler_params=pltpu.CompilerParams(
            collective_id=0, has_side_effects=True, vmem_limit_bytes=48 * 2**20
        ),
        cost_estimate=pl.CostEstimate(
            flops=8 * rows * latents * width,
            bytes_accessed=2 * (latents * width + 4 * rows * width + 5 * rows * latents),
            transcendentals=0,
        ),
    )(cut(lat_own), cut(lat_other), cut(act_own), cut(act_other), dec, bias[None])
    return [x.reshape(rows, x.shape[2]) for x in outs]


def on_device(activations, enc_weight, enc_bias, dec_weight, dec_bias):
    f32, bf16 = jnp.float32, jnp.bfloat16
    rows = activations[0]
    row_count = rows.shape[0]
    loss_scale = 1.0 / math.sqrt(row_count * lax.axis_size("tok"))
    enc, dec = enc_weight[0], dec_weight[:, 0, :]
    width = enc.shape[0]
    tok = lax.axis_index("tok")
    act_own = lax.dynamic_slice_in_dim(rows, tok * width, width, axis=1)
    act_sent = lax.dynamic_slice_in_dim(rows, (1 - tok) * width, width, axis=1)
    act_other = swap(act_sent, "tok")
    half_sq = jnp.sum(jnp.square(dec.astype(f32)), axis=1)
    dec_norms = jnp.sqrt(lax.psum(half_sq, ("layer", "tok")) + EPSILON)

    def token_terms(own, other):
        arrived = swap(other.astype(bf16), "tok")
        mine = (own + arrived.astype(f32)).astype(bf16)
        return mine.astype(f32) + swap(mine, "layer").astype(f32)

    pre_other = dot(act_other, enc, ((1,), (0,)))
    pre_own = dot(act_own, enc, ((1,), (0,)))
    preact = token_terms(pre_own, pre_other) + enc_bias
    positive = jnp.maximum(preact, 0.0)
    lat_own = (positive * positive).astype(bf16)
    lat_other = swap(lat_own, "tok")
    bias = lax.dynamic_slice_in_dim(dec_bias[0], tok * width, width, axis=0)

    err_own, err_other, back_own, back_other = error_and_back(
        lat_own, lat_other, act_own, act_other, dec, bias
    )
    back_proj = token_terms(back_own, back_other)
    grad_own = (loss_scale * (back_proj + LAMBDA * dec_norms) * 2.0 * positive).astype(bf16)
    grad_other = swap(grad_own, "tok")
    grad_enc = dot(act_own, grad_own, ((0,), (0,))) + dot(act_other, grad_other, ((0,), (0,)))
    col_totals = jnp.sum(lat_own.astype(f32), axis=0) + jnp.sum(lat_other.astype(f32), axis=0)
    grad_dec = loss_scale * (
        dot(lat_own, err_own, ((0,), (0,)))
        + dot(lat_other, err_other, ((0,), (0,)))
        + (LAMBDA * col_totals / dec_norms)[:, None] * dec.astype(f32)
    )
    return grad_enc.astype(bf16)[None], grad_dec.astype(bf16)[:, None, :]


def solution(mesh):
    placed = (
        P("layer", "tok", None),
        P("layer", "tok", "latent"),
        P("latent"),
        P("latent", "layer", "tok"),
        P("layer", None),
    )
    return jax.shard_map(
        on_device,
        mesh=mesh,
        in_specs=placed,
        out_specs=(P("layer", "tok", "latent"), P("latent", "layer", "tok")),
        check_vma=False,
    )
```

```python
import functools
import math

import jax
import jax.numpy as jnp
from jax import lax
from jax.experimental import pallas as pl
from jax.experimental.pallas import tpu as pltpu
from jax.sharding import PartitionSpec as P

LAMBDA = 1.0
EPSILON = 1e-06


def dot(a, b, dims):
    return lax.dot_general(a, b, (dims, ((), ())), preferred_element_type=jnp.float32)


def swap(x, axis):
    return lax.ppermute(x, axis, [(0, 1), (1, 0)])


def ring_kernel(
    n, pre, enc_bias, act0, act1, dec, bias,
    pre_in, lat0, lat1, err0, err1, back, back_in,
    slots, tok_out, tok_in, rs_send, rs_recv, ag_send, ag_recv, send_sems, recv_sems,
):
    lats, acts, errs = (lat0, lat1), (act0, act1), (err0, err1)
    half = n // 2
    latent, tok, layer = (lax.axis_index(name) for name in ("latent", "tok", "layer"))
    odd = lax.rem(latent, 2)
    place = lax.div(latent, 2) + odd * (n - 1 - 2 * lax.div(latent, 2))
    signs = (1 - 2 * tok, 2 * tok - 1)

    def device_at(spot):
        far = lax.div(spot, half)
        return (1 - far) * 2 * spot + far * (2 * (n - 1 - spot) + 1)

    targets = [{"latent": device_at(lax.rem(place + sign + n, n))} for sign in signs]
    core, other_layer = {"tok": 1 - tok}, {"layer": 1 - layer}

    def chunk(way, step):
        return lax.rem(place - signs[way] * step + 2 * n, n)

    def copy(src, dst, send, recv, device):
        return pltpu.make_async_remote_copy(
            src_ref=src, dst_ref=dst, send_sem=send, recv_sem=recv,
            device_id=device, device_id_type=pl.DeviceIdType.MESH,
        )

    def rs_copy(way, step):
        return copy(
            slots.at[way, step], slots.at[way, step + 1],
            rs_send.at[way, step], rs_recv.at[way, step], targets[way],
        )

    def ag_copy(way, step, held):
        return copy(
            errs[way].at[held], errs[way].at[held],
            ag_send.at[way, step], ag_recv.at[way, step], targets[way],
        )

    def swap_copy(kind, src, dst, step, device):
        return copy(src, dst, send_sems.at[kind, step], recv_sems.at[kind, step], device)

    def pre_copy(step):
        held = chunk(0, step)
        return swap_copy(0, pre.at[held], pre_in.at[held], step, other_layer)

    def lat_copy(step):
        held = chunk(0, step)
        return swap_copy(1, lat0.at[held], lat1.at[held], step, core)

    def lat_arrival(step):
        held = chunk(1, step)
        return swap_copy(1, lat0.at[held], lat1.at[held], step, core)

    def term_copy(step):
        return swap_copy(2, tok_out.at[step], tok_in.at[step], step, core)

    def back_copy(step, held):
        return swap_copy(3, back.at[held], back_in.at[held], step, other_layer)

    def encode(step):
        held = chunk(0, step)
        pre_copy(step).wait_recv()
        total = pre[held].astype(jnp.float32) + pre_in[held].astype(jnp.float32)
        positive = jnp.maximum(total + enc_bias[...], 0.0)
        lat0[held] = (positive * positive).astype(lat0.dtype)
        lat_copy(step).start()

    def partials(step):
        own = jnp.dot(lat0[chunk(0, step)], dec[...], preferred_element_type=jnp.float32)
        lat_arrival(step).wait_recv()
        other = jnp.dot(lat1[chunk(1, step)], dec[...], preferred_element_type=jnp.float32)
        return own, other

    def project(step, helds):
        other = dot(err1[helds[1]], dec[...], ((1,), (1,)))
        tok_out[step] = other.astype(tok_out.dtype)
        term_copy(step).start()
        own = dot(err0[helds[0]], dec[...], ((1,), (1,)))
        term_copy(step).wait_recv()
        back[helds[0]] = (own + tok_in[step].astype(jnp.float32)).astype(back.dtype)
        back_copy(step, helds[0]).start()

    barrier = pltpu.get_barrier_semaphore()
    for device in (*targets, core, other_layer):
        pl.semaphore_signal(
            barrier, inc=1, device_id=device, device_id_type=pl.DeviceIdType.MESH
        )
    pl.semaphore_wait(barrier, 4)

    @pl.loop(0, n)
    def _(step):
        pre_copy(step).start()

    encode(0)
    parts = partials(0)
    for way in range(2):
        slots[way, 0] = parts[way].astype(slots.dtype)
        rs_copy(way, 0).start()
    encode(1)

    @pl.loop(1, n - 1)
    def _(step):
        parts = partials(step)
        for way in range(2):
            rs_copy(way, step - 1).wait_recv()
            total = slots[way, step].astype(jnp.float32) + parts[way]
            slots[way, step] = total.astype(slots.dtype)
            rs_copy(way, step).start()
        encode(step + 1)

    parts = partials(n - 1)
    for way in range(2):
        held = chunk(way, n - 1)
        rs_copy(way, n - 2).wait_recv()
        total = slots[way, n - 1].astype(jnp.float32) + parts[way]
        error = total + bias[...] - acts[way][held].astype(jnp.float32)
        errs[way][held] = error.astype(errs[way].dtype)
        ag_copy(way, 0, held).start()
    project(0, [chunk(way, n - 1) for way in range(2)])

    @pl.loop(0, n - 1)
    def _(step):
        for way in range(2):
            ag_copy(way, step, chunk(way, step)).wait_recv()

            @pl.when(step < n - 2)
            def _():
                ag_copy(way, step + 1, chunk(way, step)).start()

        project(step + 1, [chunk(way, step) for way in range(2)])

    @pl.loop(0, n)
    def _(step):
        held = chunk(0, step - 1 + n)
        back_copy(step, held).wait_recv()
        back_copy(step, held).wait_send()
        term_copy(step).wait_send()
        pre_copy(step).wait_send()
        lat_copy(step).wait_send()

    @pl.loop(0, n - 1)
    def _(step):
        for way in range(2):
            rs_copy(way, step).wait_send()
            ag_copy(way, step, chunk(way, step - 1 + n)).wait_send()


def ring(pre, enc_bias, act_own, act_other, dec, bias):
    n = lax.axis_size("latent")
    rows, latents = pre.shape
    width = dec.shape[1]
    part = rows // n
    cut = lambda x: x.reshape(n, part, x.shape[1])
    narrow = jax.ShapeDtypeStruct((n, part, latents), jnp.bfloat16)
    wide = jax.ShapeDtypeStruct((n, part, width), jnp.bfloat16)
    ring_sems = pltpu.SemaphoreType.DMA((2, n - 1))
    swap_sems = pltpu.SemaphoreType.DMA((4, n))
    terms = pltpu.VMEM((n, part, latents), jnp.bfloat16)
    outs = pl.pallas_call(
        functools.partial(ring_kernel, n),
        out_shape=[narrow] * 3 + [wide] * 2 + [narrow] * 2,
        in_specs=[pl.BlockSpec(memory_space=pltpu.VMEM)] * 6,
        out_specs=[pl.BlockSpec(memory_space=pltpu.VMEM)] * 7,
        scratch_shapes=[pltpu.VMEM((2, n, part, width), jnp.bfloat16), terms, terms]
        + [ring_sems] * 4
        + [swap_sems] * 2,
        compiler_params=pltpu.CompilerParams(
            collective_id=0, has_side_effects=True, vmem_limit_bytes=48 * 2**20
        ),
        cost_estimate=pl.CostEstimate(
            flops=8 * rows * latents * width,
            bytes_accessed=2 * (latents * width + 4 * rows * width + 6 * rows * latents),
            transcendentals=0,
        ),
    )(cut(pre), enc_bias[None], cut(act_own), cut(act_other), dec, bias[None])
    return [x.reshape(rows, x.shape[2]) for x in outs]


def on_device(activations, enc_weight, enc_bias, dec_weight, dec_bias):
    f32, bf16 = jnp.float32, jnp.bfloat16
    rows = activations[0]
    row_count = rows.shape[0]
    loss_scale = 1.0 / math.sqrt(row_count * lax.axis_size("tok"))
    enc, dec = enc_weight[0], dec_weight[:, 0, :]
    width = enc.shape[0]
    tok = lax.axis_index("tok")
    act_own = lax.dynamic_slice_in_dim(rows, tok * width, width, axis=1)
    act_sent = lax.dynamic_slice_in_dim(rows, (1 - tok) * width, width, axis=1)
    act_other = swap(act_sent, "tok")
    half_sq = jnp.sum(jnp.square(dec.astype(f32)), axis=1)
    dec_norms = jnp.sqrt(lax.psum(half_sq, ("layer", "tok")) + EPSILON)

    pre_other = dot(act_other, enc, ((1,), (0,))).astype(bf16)
    pre_own = dot(act_own, enc, ((1,), (0,)))
    pre = (pre_own + swap(pre_other, "tok").astype(f32)).astype(bf16)
    bias = lax.dynamic_slice_in_dim(dec_bias[0], tok * width, width, axis=0)
    pre_in, lat_own, lat_other, err_own, err_other, back, back_in = ring(
        pre, enc_bias, act_own, act_other, dec, bias
    )
    positive = jnp.maximum(pre.astype(f32) + pre_in.astype(f32) + enc_bias, 0.0)
    back_proj = back.astype(f32) + back_in.astype(f32)
    grad_own = (loss_scale * (back_proj + LAMBDA * dec_norms) * 2.0 * positive).astype(bf16)
    grad_other = swap(grad_own, "tok")
    grad_enc = dot(act_own, grad_own, ((0,), (0,))) + dot(act_other, grad_other, ((0,), (0,)))
    col_totals = jnp.sum(lat_own.astype(f32), axis=0) + jnp.sum(lat_other.astype(f32), axis=0)
    grad_dec = loss_scale * (
        dot(lat_own, err_own, ((0,), (0,)))
        + dot(lat_other, err_other, ((0,), (0,)))
        + (LAMBDA * col_totals / dec_norms)[:, None] * dec.astype(f32)
    )
    return grad_enc.astype(bf16)[None], grad_dec.astype(bf16)[:, None, :]


def solution(mesh):
    placed = (
        P("layer", "tok", None),
        P("layer", "tok", "latent"),
        P("latent"),
        P("latent", "layer", "tok"),
        P("layer", None),
    )
    return jax.shard_map(
        on_device,
        mesh=mesh,
        in_specs=placed,
        out_specs=(P("layer", "tok", "latent"), P("latent", "layer", "tok")),
        check_vma=False,
    )
```

```python
import functools
import math

import jax
import jax.numpy as jnp
from jax import lax
from jax.experimental import pallas as pl
from jax.experimental.pallas import tpu as pltpu
from jax.sharding import PartitionSpec as P

LAMBDA = 1.0
EPSILON = 1e-06


def dot(a, b, dims):
    return lax.dot_general(a, b, (dims, ((), ())), preferred_element_type=jnp.float32)


def swap(x, axis):
    return lax.ppermute(x, axis, [(0, 1), (1, 0)])


def ring_kernel(
    n, pre, enc_bias, act0, act1, dec, bias, norm,
    pre_in, lat0, lat1, err0, err1, back, back_in, norm_sum,
    slots, tok_out, tok_in, norm_core, norm_chip, norm_in, rs_send, rs_recv, ag_send, ag_recv, send_sems, recv_sems,
):
    lats, acts, errs = (lat0, lat1), (act0, act1), (err0, err1)
    half = n // 2
    latent, tok, layer = (lax.axis_index(name) for name in ("latent", "tok", "layer"))
    odd = lax.rem(latent, 2)
    place = lax.div(latent, 2) + odd * (n - 1 - 2 * lax.div(latent, 2))
    signs = (1 - 2 * tok, 2 * tok - 1)

    def device_at(spot):
        far = lax.div(spot, half)
        return (1 - far) * 2 * spot + far * (2 * (n - 1 - spot) + 1)

    targets = [{"latent": device_at(lax.rem(place + sign + n, n))} for sign in signs]
    core, other_layer = {"tok": 1 - tok}, {"layer": 1 - layer}

    def chunk(way, step):
        return lax.rem(place - signs[way] * step + 2 * n, n)

    def copy(src, dst, send, recv, device):
        return pltpu.make_async_remote_copy(
            src_ref=src, dst_ref=dst, send_sem=send, recv_sem=recv,
            device_id=device, device_id_type=pl.DeviceIdType.MESH,
        )

    def rs_copy(way, step):
        return copy(
            slots.at[way, step], slots.at[way, step + 1],
            rs_send.at[way, step], rs_recv.at[way, step], targets[way],
        )

    def ag_copy(way, step, held):
        return copy(
            errs[way].at[held], errs[way].at[held],
            ag_send.at[way, step], ag_recv.at[way, step], targets[way],
        )

    def swap_copy(kind, src, dst, step, device):
        return copy(src, dst, send_sems.at[kind, step], recv_sems.at[kind, step], device)

    def pre_copy(step):
        held = chunk(0, step)
        return swap_copy(0, pre.at[held], pre_in.at[held], step, other_layer)

    def lat_copy(step):
        held = chunk(0, step)
        return swap_copy(1, lat0.at[held], lat1.at[held], step, core)

    def lat_arrival(step):
        held = chunk(1, step)
        return swap_copy(1, lat0.at[held], lat1.at[held], step, core)

    def term_copy(step):
        return swap_copy(2, tok_out.at[step], tok_in.at[step], step, core)

    def back_copy(step, held):
        return swap_copy(3, back.at[held], back_in.at[held], step, other_layer)

    def norm_copy(kind):
        if kind == 4:
            return swap_copy(4, norm, norm_core, 0, core)
        return swap_copy(5, norm_chip, norm_in, 0, other_layer)

    def encode(step):
        held = chunk(0, step)
        pre_copy(step).wait_recv()
        total = pre[held].astype(jnp.float32) + pre_in[held].astype(jnp.float32)
        positive = jnp.maximum(total + enc_bias[...], 0.0)
        lat0[held] = (positive * positive).astype(lat0.dtype)
        lat_copy(step).start()

    def partials(step):
        own = jnp.dot(lat0[chunk(0, step)], dec[...], preferred_element_type=jnp.float32)
        lat_arrival(step).wait_recv()
        other = jnp.dot(lat1[chunk(1, step)], dec[...], preferred_element_type=jnp.float32)
        return own, other

    def project(step, helds):
        other = dot(err1[helds[1]], dec[...], ((1,), (1,)))
        tok_out[step] = other.astype(tok_out.dtype)
        term_copy(step).start()
        own = dot(err0[helds[0]], dec[...], ((1,), (1,)))
        term_copy(step).wait_recv()
        back[helds[0]] = (own + tok_in[step].astype(jnp.float32)).astype(back.dtype)
        back_copy(step, helds[0]).start()

    barrier = pltpu.get_barrier_semaphore()
    for device in (*targets, core, other_layer):
        pl.semaphore_signal(
            barrier, inc=1, device_id=device, device_id_type=pl.DeviceIdType.MESH
        )
    pl.semaphore_wait(barrier, 4)
    norm_copy(4).start()

    @pl.loop(0, n)
    def _(step):
        pre_copy(step).start()

    encode(0)
    parts = partials(0)
    for way in range(2):
        slots[way, 0] = parts[way].astype(slots.dtype)
        rs_copy(way, 0).start()
    encode(1)
    norm_copy(4).wait_recv()
    norm_chip[...] = norm[...] + norm_core[...]
    norm_copy(5).start()

    @pl.loop(1, n - 1)
    def _(step):
        parts = partials(step)
        for way in range(2):
            rs_copy(way, step - 1).wait_recv()
            total = slots[way, step].astype(jnp.float32) + parts[way]
            slots[way, step] = total.astype(slots.dtype)
            rs_copy(way, step).start()
        encode(step + 1)

    parts = partials(n - 1)
    for way in range(2):
        held = chunk(way, n - 1)
        rs_copy(way, n - 2).wait_recv()
        total = slots[way, n - 1].astype(jnp.float32) + parts[way]
        error = total + bias[...] - acts[way][held].astype(jnp.float32)
        errs[way][held] = error.astype(errs[way].dtype)
        ag_copy(way, 0, held).start()
    project(0, [chunk(way, n - 1) for way in range(2)])
    norm_copy(5).wait_recv()
    norm_sum[...] = norm_chip[...] + norm_in[...]
    norm_copy(4).wait_send()
    norm_copy(5).wait_send()

    @pl.loop(0, n - 1)
    def _(step):
        for way in range(2):
            ag_copy(way, step, chunk(way, step)).wait_recv()

            @pl.when(step < n - 2)
            def _():
                ag_copy(way, step + 1, chunk(way, step)).start()

        project(step + 1, [chunk(way, step) for way in range(2)])

    @pl.loop(0, n)
    def _(step):
        held = chunk(0, step - 1 + n)
        back_copy(step, held).wait_recv()
        back_copy(step, held).wait_send()
        term_copy(step).wait_send()
        pre_copy(step).wait_send()
        lat_copy(step).wait_send()

    @pl.loop(0, n - 1)
    def _(step):
        for way in range(2):
            rs_copy(way, step).wait_send()
            ag_copy(way, step, chunk(way, step - 1 + n)).wait_send()


def ring(pre, enc_bias, act_own, act_other, dec, bias, norm):
    n = lax.axis_size("latent")
    rows, latents = pre.shape
    width = dec.shape[1]
    part = rows // n
    cut = lambda x: x.reshape(n, part, x.shape[1])
    narrow = jax.ShapeDtypeStruct((n, part, latents), jnp.bfloat16)
    wide = jax.ShapeDtypeStruct((n, part, width), jnp.bfloat16)
    ring_sems = pltpu.SemaphoreType.DMA((2, n - 1))
    swap_sems = pltpu.SemaphoreType.DMA((6, n))
    norms = pltpu.VMEM((1, latents), jnp.float32)
    terms = pltpu.VMEM((n, part, latents), jnp.bfloat16)
    outs = pl.pallas_call(
        functools.partial(ring_kernel, n),
        out_shape=[narrow] * 3 + [wide] * 2 + [narrow] * 2
        + [jax.ShapeDtypeStruct((1, latents), jnp.float32)],
        in_specs=[pl.BlockSpec(memory_space=pltpu.VMEM)] * 7,
        out_specs=[pl.BlockSpec(memory_space=pltpu.VMEM)] * 8,
        scratch_shapes=[pltpu.VMEM((2, n, part, width), jnp.bfloat16), terms, terms]
        + [norms] * 3
        + [ring_sems] * 4
        + [swap_sems] * 2,
        compiler_params=pltpu.CompilerParams(
            collective_id=0, has_side_effects=True, vmem_limit_bytes=48 * 2**20
        ),
        cost_estimate=pl.CostEstimate(
            flops=8 * rows * latents * width,
            bytes_accessed=2 * (latents * width + 4 * rows * width + 6 * rows * latents),
            transcendentals=0,
        ),
    )(cut(pre), enc_bias[None], cut(act_own), cut(act_other), dec, bias[None], norm[None])
    return [x.reshape(rows, x.shape[2]) for x in outs[:-1]] + [outs[-1][0]]


def on_device(activations, enc_weight, enc_bias, dec_weight, dec_bias):
    f32, bf16 = jnp.float32, jnp.bfloat16
    rows = activations[0]
    row_count = rows.shape[0]
    loss_scale = 1.0 / math.sqrt(row_count * lax.axis_size("tok"))
    enc, dec = enc_weight[0], dec_weight[:, 0, :]
    width = enc.shape[0]
    tok = lax.axis_index("tok")
    act_own = lax.dynamic_slice_in_dim(rows, tok * width, width, axis=1)
    act_sent = lax.dynamic_slice_in_dim(rows, (1 - tok) * width, width, axis=1)
    act_other = swap(act_sent, "tok")
    half_sq = jnp.sum(jnp.square(dec.astype(f32)), axis=1)

    pre_other = dot(act_other, enc, ((1,), (0,))).astype(bf16)
    pre_own = dot(act_own, enc, ((1,), (0,)))
    pre = (pre_own + swap(pre_other, "tok").astype(f32)).astype(bf16)
    bias = lax.dynamic_slice_in_dim(dec_bias[0], tok * width, width, axis=0)
    pre_in, lat_own, lat_other, err_own, err_other, back, back_in, norm_sq = ring(
        pre, enc_bias, act_own, act_other, dec, bias, half_sq
    )
    dec_norms = jnp.sqrt(norm_sq + EPSILON)
    positive = jnp.maximum(pre.astype(f32) + pre_in.astype(f32) + enc_bias, 0.0)
    back_proj = back.astype(f32) + back_in.astype(f32)
    grad_own = (loss_scale * (back_proj + LAMBDA * dec_norms) * 2.0 * positive).astype(bf16)
    grad_other = swap(grad_own, "tok")
    grad_enc = dot(act_own, grad_own, ((0,), (0,))) + dot(act_other, grad_other, ((0,), (0,)))
    col_totals = jnp.sum(lat_own.astype(f32), axis=0) + jnp.sum(lat_other.astype(f32), axis=0)
    grad_dec = loss_scale * (
        dot(lat_own, err_own, ((0,), (0,)))
        + dot(lat_other, err_other, ((0,), (0,)))
        + (LAMBDA * col_totals / dec_norms)[:, None] * dec.astype(f32)
    )
    return grad_enc.astype(bf16)[None], grad_dec.astype(bf16)[:, None, :]


def solution(mesh):
    placed = (
        P("layer", "tok", None),
        P("layer", "tok", "latent"),
        P("latent"),
        P("latent", "layer", "tok"),
        P("layer", None),
    )
    return jax.shard_map(
        on_device,
        mesh=mesh,
        in_specs=placed,
        out_specs=(P("layer", "tok", "latent"), P("latent", "layer", "tok")),
        check_vma=False,
    )
```
